32 devices in a mesh: lon: 8 (over z, x), lat: 4 (over y, core).
Axes of the slice: x: 2, y: 2, z: 4, core: 2. Of those that a mesh axis runs over, the one named last changes fastest.
Arguments:
- adj_u: float32 [8, 32, 8192], P(None, 'lat', 'lon'), may hold values from -6 to 6
- adj_v: float32 [8, 32, 8192], P(None, 'lat', 'lon'), may hold values from -6 to 6
- adj_zeta: float32 [32, 8192], P('lat', 'lon'), may hold values from -6 to 6
- saved_zeta: float32 [20, 32, 8192], P(None, 'lat', 'lon'), may hold values from -1 to 1
- saved_ubar: float32 [20, 32, 8192], P(None, 'lat', 'lon'), may hold values from -3 to 3
- stored_mean_north_velocity: float32 [20, 32, 8192], P(None, 'lat', 'lon'), may hold values from -3 to 3
- depth: float32 [32, 8192], P('lat', 'lon'), may hold values from 0.5 to 1.5
- scaled_inverse_area: float32 [32, 8192], P('lat', 'lon'), may hold values from 0.5 to 1.5
- level_base: float32 [8], replicated, may hold values from 0.05 to 0.3
- level_slope: float32 [8], replicated, may hold values from 0.05 to 0.3
- rho_mask: int32 [32, 8192], P('lat', 'lon'), may hold values 0 or 1
- u_mask: int32 [32, 8192], P('lat', 'lon'), may hold values 0 or 1
- v_mask: int32 [32, 8192], P('lat', 'lon'), may hold values 0 or 1
- filter_table: float32 [32], replicated, may hold values from 0.2 to 2
- filter_index: int32 [20], replicated, may hold values from 0 to 31
Outputs:
- adj_zeta0: float32 [32, 8192], P('lat', 'lon')
- adj_ubar0: float32 [32, 8192], P('lat', 'lon')
- adj_vbar0: float32 [32, 8192], P('lat', 'lon')
- adj_u3: float32 [8, 32, 8192], P(None, 'lat', 'lon')
- adj_v3: float32 [8, 32, 8192], P(None, 'lat', 'lon')
The draws below stay inside these ranges and needn't reach their ends.
All inputs are finite; a program needn't handle non-finite values. No bound on the sum of `rho_mask` or of `u_mask` or of `v_mask` on one device may be relied on, other than what follows from the above.
Results may differ from the reference program's by a relative error of at most 0.00002.
Values sent between devices are 32-bit elements; how exact they have to be, the bound alone decides.
A program may use at most 64 MiB of HBM per device.

```python
import math
import jax
import jax.numpy as jnp
from jax import lax

NZ = 8
NSUB = 20
NFILT = 32
NY = 32
NX = 8192


def with_ends(entries, own_key, smallest, high):
    place = [jax.random.randint(jax.random.fold_in(own_key, axis), (), 0, length) for axis, length in enumerate(entries.shape)]
    main_axis = entries.shape.index(max(entries.shape))
    neighbour = place[:main_axis] + [(place[main_axis] + 1) % entries.shape[main_axis]] + place[main_axis + 1:]
    return entries.at[tuple(place)].set(smallest).at[tuple(neighbour)].set(high)


def shard_levels(rng, extent, pieces, smallest, largest):
    loudness, own = 1.0, jax.random.fold_in(rng, 6)
    for position, shards_of in pieces:
        heights = jnp.exp(jax.random.uniform(jax.random.fold_in(own, position), (shards_of,), jnp.float32, smallest / len(pieces), largest / len(pieces)))
        loudness = loudness * jnp.repeat(heights, extent[position] // shards_of).reshape([-1 if axis == position else 1 for axis in range(len(extent))])
    return loudness


def normal_values(stream_key, dims, width, reach, shards=(), held_as=jnp.bfloat16):
    level = shard_levels(stream_key, dims, shards, -0.22, 0.18) if shards else 1.0
    drawn = jax.random.normal(stream_key, dims, jnp.float32) * width * level
    return jnp.minimum(jnp.maximum(drawn, -reach), reach).astype(held_as)


def setup_inputs(seed: int = 0) -> dict:
    streams_of = jax.random.split(jax.random.key(seed), 16)
    return {
        "adj_u": normal_values(streams_of[0], (NZ, NY, NX), 1.0, 6.0, ((1, 4), (2, 8)), jnp.float32),
        "adj_v": normal_values(streams_of[1], (NZ, NY, NX), 1.0, 6.0, ((1, 4), (2, 8)), jnp.float32),
        "adj_zeta": normal_values(streams_of[2], (NY, NX), 1.0, 6.0, ((0, 4), (1, 8)), jnp.float32),
        "saved_zeta": normal_values(streams_of[3], (NSUB, NY, NX), 0.2, 1.0, ((1, 4), (2, 8)), jnp.float32),
        "saved_ubar": normal_values(streams_of[4], (NSUB, NY, NX), 0.5, 3.0, ((1, 4), (2, 8)), jnp.float32),
        "stored_mean_north_velocity": normal_values(streams_of[5], (NSUB, NY, NX), 0.5, 3.0, ((1, 4), (2, 8)), jnp.float32),
        "depth": jnp.clip(jnp.exp(math.log(1.5) - 1.0986123 * jax.random.uniform(streams_of[6], (NY, NX), jnp.float32) ** shard_levels(streams_of[6], (NY, NX), ((0, 4), (1, 8)), -0.2, 0.2)), 0.5, 1.5),
        "scaled_inverse_area": jnp.clip(jnp.exp(math.log(1.5) - 1.0986123 * jax.random.uniform(streams_of[7], (NY, NX), jnp.float32) ** shard_levels(streams_of[7], (NY, NX), ((0, 4), (1, 8)), -0.2, 0.2)), 0.5, 1.5),
        "level_base": jnp.clip(jnp.exp(jax.random.uniform(streams_of[8], (NZ,), jnp.float32, math.log(0.05), math.log(0.3))), 0.05, 0.3),
        "level_slope": jnp.clip(jnp.exp(jax.random.uniform(streams_of[9], (NZ,), jnp.float32, math.log(0.05), math.log(0.3))), 0.05, 0.3),
        "rho_mask": with_ends((jax.random.randint(streams_of[10], (NY, NX), 0, 10) < 9).astype(jnp.int32), jax.random.fold_in(streams_of[10], 1), 0, 1),
        "u_mask": with_ends((jax.random.randint(streams_of[11], (NY, NX), 0, 10) < 9).astype(jnp.int32), jax.random.fold_in(streams_of[11], 1), 0, 1),
        "v_mask": with_ends((jax.random.randint(streams_of[12], (NY, NX), 0, 10) < 9).astype(jnp.int32), jax.random.fold_in(streams_of[12], 1), 0, 1),
        "filter_table": jnp.clip(jnp.exp(jax.random.uniform(streams_of[13], (NFILT,), jnp.float32, math.log(0.2), math.log(2.0))), 0.2, 2.0),
        "filter_index": with_ends(jax.random.randint(streams_of[14], (NSUB,), 0, NFILT), jax.random.fold_in(streams_of[14], 1), 0, NFILT - 1).astype(jnp.int32),
    }


flux_scale = 0.3
slope_scale = 0.3
keep_rate = 0.98

def mass_balance(elevation_with_halo, mean_east_velocity_halo, mean_north_velocity_halo, stored_elevation_halo, stored_east_velocity_halo, stored_north_velocity_halo, depth_with_halo, east_mask_halo, north_mask_halo, tracer_land_mask, scaled_inverse_area):
    zeta_east = 0.5 * (elevation_with_halo[1:-1, :-1] + elevation_with_halo[1:-1, 1:])
    depth_east = 0.5 * (depth_with_halo[1:-1, :-1] + depth_with_halo[1:-1, 1:] + stored_elevation_halo[1:-1, :-1] + stored_elevation_halo[1:-1, 1:])
    flux_east = east_mask_halo[1:-1, 1:] * (depth_east * mean_east_velocity_halo[1:-1, 1:] + stored_east_velocity_halo[1:-1, 1:] * zeta_east)
    northward_elevation = 0.5 * (elevation_with_halo[:-1, 1:-1] + elevation_with_halo[1:, 1:-1])
    northward_depth = 0.5 * (depth_with_halo[:-1, 1:-1] + depth_with_halo[1:, 1:-1] + stored_elevation_halo[:-1, 1:-1] + stored_elevation_halo[1:, 1:-1])
    northward_flux = north_mask_halo[1:, 1:-1] * (northward_depth * mean_north_velocity_halo[1:, 1:-1] + stored_north_velocity_halo[1:, 1:-1] * northward_elevation)
    spread = flux_east[:, 1:] - flux_east[:, :-1] + northward_flux[1:, :] - northward_flux[:-1, :]
    return elevation_with_halo[1:-1, 1:-1] - flux_scale * tracer_land_mask * scaled_inverse_area * spread

def momentum(elevation_with_halo, mean_east_velocity, mean_north_velocity, u_land, north_land_mask):
    slope_east = elevation_with_halo[1:-1, 1:-1] - elevation_with_halo[1:-1, :-2]
    slope_north = elevation_with_halo[1:-1, 1:-1] - elevation_with_halo[:-2, 1:-1]
    return (u_land * (keep_rate * mean_east_velocity - slope_scale * slope_east), north_land_mask * (keep_rate * mean_north_velocity - slope_scale * slope_north))

def periodic_halo_fill(field):
    field = jnp.concatenate([field[..., -1:], field, field[..., :1]], axis=-1)
    edge_zero = jnp.zeros(field.shape[:-2] + (1, field.shape[-1]), jnp.float32)
    return jnp.concatenate([edge_zero, field, edge_zero], axis=-2)

def reference(adj_u, adj_v, adj_zeta, saved_zeta, saved_ubar, stored_mean_north_velocity, depth, scaled_inverse_area, level_base, level_slope, rho_mask, u_mask, v_mask, filter_table, filter_index):
    tracer_land_mask = rho_mask.astype(jnp.float32)
    u_land = u_mask.astype(jnp.float32)
    row_ids = jnp.arange(NY, dtype=jnp.int32)
    north_land_mask = v_mask.astype(jnp.float32) * (row_ids > 0).astype(jnp.float32)[:, None]
    depth_with_halo = periodic_halo_fill(depth)
    east_mask_halo = periodic_halo_fill(u_land)
    north_mask_halo = periodic_halo_fill(north_land_mask)
    raw_weights = filter_table[filter_index]
    weights = raw_weights / jnp.sum(raw_weights)
    thick = level_base[:, None, None] + level_slope[:, None, None] * depth[None]
    total = lax.optimization_barrier(jnp.sum(thick, axis=0))
    sum_u = lax.optimization_barrier(jnp.sum(adj_u, axis=0))
    sum_v = lax.optimization_barrier(jnp.sum(adj_v, axis=0))
    adj_u3 = adj_u - thick / total[None] * sum_u[None]
    adj_v3 = adj_v - thick / total[None] * sum_v[None]
    zero_field = jnp.zeros((NY, NX), jnp.float32)
    back_zeta, back_ubar, backward_mean_north_velocity = (zero_field, zero_field, zero_field)
    for inner_step_index in reversed(range(NSUB)):
        stored_elevation_halo = periodic_halo_fill(saved_zeta[inner_step_index])
        stored_east_velocity_halo = periodic_halo_fill(saved_ubar[inner_step_index])
        stored_north_velocity_halo = periodic_halo_fill(stored_mean_north_velocity[inner_step_index])
        weight = weights[inner_step_index]
        back_zeta = back_zeta + weight * adj_zeta
        back_ubar = back_ubar + weight * sum_u
        backward_mean_north_velocity = backward_mean_north_velocity + weight * sum_v

        def move_fn(surface_elevation, mean_east_velocity, mean_north_velocity):
            return momentum(periodic_halo_fill(surface_elevation), mean_east_velocity, mean_north_velocity, u_land, north_land_mask)
        _, pull = jax.vjp(move_fn, zero_field, zero_field, zero_field)
        part_zeta, part_ubar, part_vbar = pull((back_ubar, backward_mean_north_velocity))
        back_zeta = back_zeta + part_zeta

        def spread_fn(surface_elevation, mean_east_velocity, mean_north_velocity):
            return mass_balance(periodic_halo_fill(surface_elevation), periodic_halo_fill(mean_east_velocity), periodic_halo_fill(mean_north_velocity), stored_elevation_halo, stored_east_velocity_halo, stored_north_velocity_halo, depth_with_halo, east_mask_halo, north_mask_halo, tracer_land_mask, scaled_inverse_area)
        _, pull = jax.vjp(spread_fn, zero_field, zero_field, zero_field)
        more_zeta, more_ubar, more_vbar = pull(back_zeta)
        back_zeta = more_zeta
        back_ubar = part_ubar + more_ubar
        backward_mean_north_velocity = part_vbar + more_vbar
    return (back_zeta, back_ubar, backward_mean_north_velocity, adj_u3, adj_v3)
```

```python
import functools

import jax
import jax.numpy as jnp
from jax import lax
from jax.experimental import pallas as pl
from jax.experimental.pallas import tpu as pltpu
from jax.sharding import PartitionSpec as P

SBLOCK = 4
EDGE = 32
LANES = 128

flux_scale = 0.3
slope_scale = 0.3
keep_rate = 0.98
MESH = pl.DeviceIdType.MESH


def rolled(values, shift, axis):
    return pltpu.roll(values, shift % values.shape[axis], axis)


def east_of(values):
    return rolled(values, -1, 1)


def west_of(values):
    return rolled(values, 1, 1)


def north_of(values):
    return rolled(values, -1, 0)


def south_of(values):
    return rolled(values, 1, 0)


def kernel(
    lon_count,
    lat_count,
    adj_u_hbm,
    adj_v_hbm,
    adj_zeta_hbm,
    saved_z_hbm,
    saved_u_hbm,
    saved_v_hbm,
    depth_hbm,
    area_hbm,
    rho_hbm,
    um_hbm,
    vm_hbm,
    level_base,
    level_slope,
    filter_table,
    filter_index,
    out_z,
    out_u,
    out_v,
    out_u3,
    out_v3,
    adj_u,
    adj_v,
    adj_zeta,
    depth,
    area,
    rho,
    um,
    vm,
    own_z,
    own_u,
    own_v,
    halo_z,
    halo_u,
    halo_v,
    static,
    halo_static,
    pack_west,
    pack_east,
    from_east,
    from_west,
    halo_east,
    halo_west,
    state_out,
    halo_state,
    state,
    ring,
    local_sem,
    bulk_send,
    bulk_recv,
    static_send,
    static_recv,
    lon_send,
    lon_recv,
    forward_send,
    forward_recv,
    state_send,
    state_recv,
):
    substeps, rows, columns = saved_z_hbm.shape
    levels = adj_u_hbm.shape[0]
    half = rows // 2
    wide = columns + LANES
    blocks = substeps // SBLOCK
    lon = lax.axis_index("lon")
    lat = lax.axis_index("lat")
    east = lax.rem(lon + 1, lon_count)
    west = lax.rem(lon + lon_count - 1, lon_count)
    has_north = lat < lat_count - 1
    has_south = lat > 0
    main = pl.ds(0, columns)
    side = pl.ds(columns, LANES)
    saved_hbm = (saved_z_hbm, saved_u_hbm, saved_v_hbm)
    own = (own_z, own_u, own_v)
    halo = (halo_z, halo_u, halo_v)

    small = (
        (adj_u_hbm, adj_u),
        (adj_v_hbm, adj_v),
        (adj_zeta_hbm, adj_zeta),
        (depth_hbm, depth),
        (area_hbm, area),
        (rho_hbm, rho),
        (um_hbm, um),
        (vm_hbm, vm),
    )
    small_copies = [
        pltpu.make_async_copy(src, dst, local_sem.at[i]) for i, (src, dst) in enumerate(small)
    ]
    split = substeps - SBLOCK
    saved_copies = []
    for part, (low, count) in enumerate(((split, SBLOCK), (0, split))):
        saved_copies.append(
            [
                pltpu.make_async_copy(
                    saved_hbm[f].at[pl.ds(low, count)],
                    own[f].at[pl.ds(low, count), :, main],
                    local_sem.at[8 + 3 * part + f],
                )
                for f in range(3)
            ]
        )
    for copy in small_copies + saved_copies[0] + saved_copies[1]:
        copy.start()

    for target in (halo_z, halo_u, halo_v, halo_static, halo_east, halo_west, halo_state):
        target[...] = jnp.zeros_like(target)

    barrier = pltpu.get_barrier_semaphore()
    pl.semaphore_signal(barrier, inc=1, device_id={"lon": east}, device_id_type=MESH)
    pl.semaphore_signal(barrier, inc=1, device_id={"lon": west}, device_id_type=MESH)

    @pl.when(has_north)
    def _():
        pl.semaphore_signal(barrier, inc=1, device_id={"lat": lat + 1}, device_id_type=MESH)

    @pl.when(has_south)
    def _():
        pl.semaphore_signal(barrier, inc=1, device_id={"lat": lat - 1}, device_id_type=MESH)

    pl.semaphore_wait(
        barrier, 2 + jnp.minimum(lat, 1) + jnp.minimum(lat_count - 1 - lat, 1)
    )

    def lat_copy(src, dst, sends, recvs, northward):
        return pltpu.make_async_remote_copy(
            src_ref=src,
            dst_ref=dst,
            send_sem=sends,
            recv_sem=recvs,
            device_id={"lat": lat + 1 if northward else lat - 1},
            device_id_type=MESH,
        )

    def bulk(block, northward):
        copies = []
        for inner in range(SBLOCK):
            reach = SBLOCK - inner
            n = substeps - 1 - block * SBLOCK - inner
            counts = (reach, reach - 1, reach - 1 if northward else reach)
            for f in range(3):
                if counts[f] == 0:
                    continue
                at = pl.ds(rows - counts[f] if northward else 0, counts[f])
                place = (int(northward), block, len(copies))
                copies.append(
                    lat_copy(
                        saved_hbm[f].at[n, at, :],
                        halo[f].at[n, at, main],
                        bulk_send.at[place],
                        bulk_recv.at[place],
                        northward,
                    )
                )
        return copies

    def halves(northward):
        return pl.ds(half, half) if northward else pl.ds(0, half)

    def static_copies(northward):
        at = halves(northward)
        return [
            lat_copy(
                static.at[:, at, main],
                halo_static.at[:, at, main],
                static_send.at[int(northward)],
                static_recv.at[int(northward)],
                northward,
            )
        ]

    groups = pack_west.shape[0]
    first = 2 + 3
    pieces = (pl.ds(0, first), pl.ds(first, groups - first))

    def lon_copies(part):
        at = pieces[part]
        return [
            pltpu.make_async_remote_copy(
                src_ref=src.at[at],
                dst_ref=dst.at[at],
                send_sem=lon_send.at[part, way],
                recv_sem=lon_recv.at[part, way],
                device_id={"lon": target},
                device_id_type=MESH,
            )
            for way, (src, dst, target) in enumerate(
                ((pack_west, from_east, west), (pack_east, from_west, east))
            )
        ]

    def forward_copies(part, northward):
        at = halves(northward)
        return [
            lat_copy(
                src.at[pieces[part], at, :],
                dst.at[pieces[part], at, :],
                forward_send.at[part, int(northward), way],
                forward_recv.at[part, int(northward), way],
                northward,
            )
            for way, (src, dst) in enumerate(((from_east, halo_east), (from_west, halo_west)))
        ]

    def state_copies(block, northward):
        at = halves(northward)
        return [
            lat_copy(
                state_out.at[block, :, at, :],
                halo_state.at[block, :, at, :],
                state_send.at[block, int(northward)],
                state_recv.at[block, int(northward)],
                northward,
            )
        ]

    def start_lat(make):
        for northward, there in ((False, has_south), (True, has_north)):

            @pl.when(there)
            def _():
                for copy in make(northward):
                    copy.start()

    def wait_lat_recv(make):
        for northward, there in ((True, has_south), (False, has_north)):

            @pl.when(there)
            def _():
                for copy in make(northward):
                    copy.wait_recv()

    def wait_lat_send(make):
        for northward, there in ((False, has_south), (True, has_north)):

            @pl.when(there)
            def _():
                for copy in make(northward):
                    copy.wait_send()

    start_lat(functools.partial(bulk, 0))

    raw_sum = filter_table[filter_index[0]]
    for n in range(1, substeps):
        raw_sum = raw_sum + filter_table[filter_index[n]]

    def raw_weight(n):
        return filter_table[filter_index[n]]

    for copy in small_copies:
        copy.wait()
    inverse = 1.0 / jnp.full((rows, columns), raw_sum, jnp.float32)
    deep = depth[...]
    sum_u = jnp.sum(adj_u[...], axis=0)
    sum_v = jnp.sum(adj_v[...], axis=0)
    row_ids = lax.broadcasted_iota(jnp.int32, (rows, columns), 0)
    north_mask = jnp.where((row_ids == 0) & (lat == 0), 0.0, vm[...].astype(jnp.float32))
    cot_v = sum_v * inverse
    static[0, :, main] = deep
    static[1, :, main] = -flux_scale * rho[...].astype(jnp.float32) * area[...]
    static[2, :, main] = um[...].astype(jnp.float32)
    static[3, :, main] = north_mask
    static[4, :, main] = adj_zeta[...] * inverse
    static[5, :, main] = sum_u * inverse
    static[6, :, main] = cot_v

    def lacking(grad_north):
        ids = lax.broadcasted_iota(jnp.int32, grad_north.shape, 0)
        return jnp.where(ids == half - 1, slope_scale * north_of(grad_north), 0.0)

    static[7, :, main] = lacking(north_mask * (raw_weight(substeps - 1) * cot_v))
    start_lat(static_copies)

    quarter = lax.broadcasted_iota(jnp.int32, (rows, LANES), 1) // EDGE

    def pack(group, refs):
        to_west = refs[0][:, pl.ds(0, LANES)]
        to_east = refs[0][:, pl.ds(columns - LANES, LANES)]
        for q in range(1, 4):
            to_west = jnp.where(
                quarter == q, rolled(refs[q][:, pl.ds(0, LANES)], EDGE * q, 1), to_west
            )
            to_east = jnp.where(
                quarter == (q + 3) % 4,
                rolled(refs[q][:, pl.ds(columns - LANES, LANES)], EDGE * q, 1),
                to_east,
            )
        pack_west[group] = to_west
        pack_east[group] = to_east

    def unpack(group, targets, east_ref, west_ref):
        for q in range(4):
            both = jnp.where(quarter == q, east_ref[group], west_ref[group])
            both = rolled(both, -EDGE * q, 1)
            targets[q][:, side] = jnp.where((quarter == 0) | (quarter == 3), both, 0.0)

    def block_fields(block, refs):
        top = substeps - 1 - block * SBLOCK
        return [refs[k % 3].at[top - k // 3] for k in range(3 * SBLOCK)]

    def pack_block(block):
        fields = block_fields(block, own)
        for g in range(3):
            pack(2 + 3 * block + g, fields[4 * g : 4 * g + 4])

    def unpack_block(block):
        for refs, east_ref, west_ref in (
            (own, from_east, from_west),
            (halo, halo_east, halo_west),
        ):
            fields = block_fields(block, refs)
            for g in range(3):
                unpack(2 + 3 * block + g, fields[4 * g : 4 * g + 4], east_ref, west_ref)

    for g in range(2):
        pack(g, [static.at[4 * g + q] for q in range(4)])
    for copy in saved_copies[0]:
        copy.wait()
    pack_block(0)
    for copy in lon_copies(0):
        copy.start()
    for copy in saved_copies[1]:
        copy.wait()

    def pack_turn(block, carry):
        pack_block(block)
        return carry

    lax.fori_loop(1, blocks, pack_turn, 0)
    for copy in lon_copies(1):
        copy.start()
    start_lat(functools.partial(bulk, 1))

    total = level_base[0] + level_slope[0] * deep
    for k in range(1, levels):
        total = total + (level_base[k] + level_slope[k] * deep)
    share_u = sum_u / total
    share_v = sum_v / total
    for k in range(levels):
        thick = level_base[k] + level_slope[k] * deep
        out_u3[k] = adj_u[k] - thick * share_u
        out_v3[k] = adj_v[k] - thick * share_v

    for copy in lon_copies(0):
        copy.wait_recv()
    start_lat(functools.partial(forward_copies, 0))
    for copy in lon_copies(1):
        copy.wait_recv()
    start_lat(functools.partial(forward_copies, 1))

    wait_lat_recv(static_copies)
    wait_lat_recv(functools.partial(forward_copies, 0))
    for refs, east_ref, west_ref in (
        (static, from_east, from_west),
        (halo_static, halo_east, halo_west),
    ):
        for g in range(2):
            unpack(g, [refs.at[4 * g + q] for q in range(4)], east_ref, west_ref)
    unpack_block(0)

    def both(own_ref, halo_ref, index):
        return jnp.concatenate([own_ref[index], halo_ref[index]], axis=0)

    deep = both(static, halo_static, 0)
    ring[0] = 0.5 * (deep + west_of(deep))
    ring[1] = 0.5 * (deep + south_of(deep))
    for k in range(1, 7):
        ring[1 + k] = both(static, halo_static, k)
    for k in range(3):
        state[k, pl.ds(0, rows), :] = jnp.zeros((rows, wide), jnp.float32)
        state[k, pl.ds(rows, rows), :] = jnp.zeros((rows, wide), jnp.float32)
    state[0, pl.ds(rows, rows), :] = halo_static[7]

    seam = lax.broadcasted_iota(jnp.int32, (2 * rows, wide), 0) == rows + half - 1

    def substep(n):
        weight = raw_weight(n)
        east_mask, north_mask = ring[3], ring[4]
        grad_east = east_mask * (state[1] + weight * ring[6])
        grad_north = north_mask * (state[2] + weight * ring[7])
        zeta_total = (state[0] + weight * ring[5]) - slope_scale * (
            grad_east
            - east_of(grad_east)
            + grad_north
            - jnp.where(seam, 0.0, north_of(grad_north))
        )
        flux = ring[2] * zeta_total
        pull_east = east_mask * (west_of(flux) - flux)
        pull_north = north_mask * (south_of(flux) - flux)
        carry_east = both(own_u, halo_u, n) * pull_east
        carry_north = both(own_v, halo_v, n) * pull_north
        saved = both(own_z, halo_z, n)
        state[0] = zeta_total + 0.5 * (
            carry_east + east_of(carry_east) + carry_north + north_of(carry_north)
        )
        state[1] = keep_rate * grad_east + (ring[0] + 0.5 * (saved + west_of(saved))) * pull_east
        state[2] = (
            keep_rate * grad_north + (ring[1] + 0.5 * (saved + south_of(saved))) * pull_north
        )

    top = pl.ds(0, rows)
    for block in range(blocks):
        wait_lat_recv(functools.partial(bulk, block))
        if block > 0:
            wait_lat_recv(functools.partial(state_copies, block - 1))
            for k in range(3):
                state[k, pl.ds(rows, rows), :] = halo_state[block - 1, k]

        def turn(inner, carry, block=block):
            substep(substeps - 1 - block * SBLOCK - inner)
            return carry

        lax.fori_loop(0, SBLOCK, turn, 0)
        if block < blocks - 1:
            weight = raw_weight(substeps - 1 - (block + 1) * SBLOCK)
            back_v = state[2, top, :]
            state_out[block, 0] = state[0, top, :] + lacking(
                ring[4, top, :] * (back_v + weight * ring[7, top, :])
            )
            state_out[block, 1] = state[1, top, :]
            state_out[block, 2] = back_v
            start_lat(functools.partial(state_copies, block))
            if block + 2 < blocks:
                start_lat(functools.partial(bulk, block + 2))
            if block == 0:
                wait_lat_recv(functools.partial(forward_copies, 1))

                def unpack_turn(index, carry):
                    unpack_block(index)
                    return carry

                lax.fori_loop(1, blocks, unpack_turn, 0)

    out_z[...] = state[0, top, main]
    out_u[...] = state[1, top, main]
    out_v[...] = state[2, top, main]

    for part in range(2):
        for copy in lon_copies(part):
            copy.wait_send()
        wait_lat_send(functools.partial(forward_copies, part))
    wait_lat_send(static_copies)
    for block in range(blocks):
        wait_lat_send(functools.partial(bulk, block))
        if block < blocks - 1:
            wait_lat_send(functools.partial(state_copies, block))


def body(
    lon_count,
    lat_count,
    adj_u,
    adj_v,
    adj_zeta,
    saved_zeta,
    saved_ubar,
    stored_mean_north_velocity,
    depth,
    scaled_inverse_area,
    level_base,
    level_slope,
    rho_mask,
    u_mask,
    v_mask,
    filter_table,
    filter_index,
):
    rows, columns = depth.shape
    substeps = saved_zeta.shape[0]
    levels = adj_u.shape[0]
    blocks = substeps // SBLOCK
    wide = columns + LANES
    groups = 2 + 3 * blocks
    most = 3 * SBLOCK
    f32, i32 = jnp.float32, jnp.int32
    flat = jax.ShapeDtypeStruct((rows, columns), f32)
    tall = jax.ShapeDtypeStruct((levels, rows, columns), f32)
    saved = pltpu.VMEM((substeps, rows, wide), f32)
    packed = pltpu.VMEM((groups, rows, LANES), f32)
    dma = pltpu.SemaphoreType.DMA
    hbm = pl.BlockSpec(memory_space=pl.ANY)
    smem = pl.BlockSpec(memory_space=pltpu.SMEM)
    vmem = pl.BlockSpec(memory_space=pltpu.VMEM)
    return pl.pallas_call(
        functools.partial(kernel, lon_count, lat_count),
        out_shape=(flat, flat, flat, tall, tall),
        in_specs=[hbm] * 11 + [smem] * 4,
        out_specs=(vmem,) * 5,
        scratch_shapes=[
            pltpu.VMEM((levels, rows, columns), f32),
            pltpu.VMEM((levels, rows, columns), f32),
            pltpu.VMEM((rows, columns), f32),
            pltpu.VMEM((rows, columns), f32),
            pltpu.VMEM((rows, columns), f32),
            pltpu.VMEM((rows, columns), i32),
            pltpu.VMEM((rows, columns), i32),
            pltpu.VMEM((rows, columns), i32),
            saved,
            saved,
            saved,
            saved,
            saved,
            saved,
            pltpu.VMEM((8, rows, wide), f32),
            pltpu.VMEM((8, rows, wide), f32),
            packed,
            packed,
            packed,
            packed,
            packed,
            packed,
            pltpu.VMEM((blocks - 1, 3, rows, wide), f32),
            pltpu.VMEM((blocks - 1, 3, rows, wide), f32),
            pltpu.VMEM((3, 2 * rows, wide), f32),
            pltpu.VMEM((8, 2 * rows, wide), f32),
            dma((14,)),
            dma((2, blocks, most)),
            dma((2, blocks, most)),
            dma((2,)),
            dma((2,)),
            dma((2, 2)),
            dma((2, 2)),
            dma((2, 2, 2)),
            dma((2, 2, 2)),
            dma((blocks - 1, 2)),
            dma((blocks - 1, 2)),
        ],
        compiler_params=pltpu.CompilerParams(
            collective_id=0, has_side_effects=True, vmem_limit_bytes=32 * 1024 * 1024
        ),
    )(
        adj_u,
        adj_v,
        adj_zeta,
        saved_zeta,
        saved_ubar,
        stored_mean_north_velocity,
        depth,
        scaled_inverse_area,
        rho_mask,
        u_mask,
        v_mask,
        level_base,
        level_slope,
        filter_table,
        filter_index,
    )


def solution(mesh):
    placed = (
        P(None, "lat", "lon"),
        P(None, "lat", "lon"),
        P("lat", "lon"),
        P(None, "lat", "lon"),
        P(None, "lat", "lon"),
        P(None, "lat", "lon"),
        P("lat", "lon"),
        P("lat", "lon"),
        P(),
        P(),
        P("lat", "lon"),
        P("lat", "lon"),
        P("lat", "lon"),
        P(),
        P(),
    )
    return jax.shard_map(
        functools.partial(body, mesh.shape["lon"], mesh.shape["lat"]),
        mesh=mesh,
        in_specs=placed,
        out_specs=(
            P("lat", "lon"),
            P("lat", "lon"),
            P("lat", "lon"),
            P(None, "lat", "lon"),
            P(None, "lat", "lon"),
        ),
        check_vma=False,
    )
```

```python
import functools

import jax
import jax.numpy as jnp
from jax import lax
from jax.experimental import pallas as pl
from jax.experimental.pallas import tpu as pltpu
from jax.sharding import PartitionSpec as P

SBLOCK = 4
EDGE = 32
LANES = 128

flux_scale = 0.3
slope_scale = 0.3
keep_rate = 0.98
MESH = pl.DeviceIdType.MESH


def rolled(values, shift, axis):
    return pltpu.roll(values, shift % values.shape[axis], axis)


def east_of(values):
    return rolled(values, -1, 1)


def west_of(values):
    return rolled(values, 1, 1)


def north_of(values):
    return rolled(values, -1, 0)


def south_of(values):
    return rolled(values, 1, 0)


def kernel(
    lon_count,
    lat_count,
    adj_u_hbm,
    adj_v_hbm,
    adj_zeta_hbm,
    saved_z_hbm,
    saved_u_hbm,
    saved_v_hbm,
    depth_hbm,
    area_hbm,
    rho_hbm,
    um_hbm,
    vm_hbm,
    base_hbm,
    slope_hbm,
    table_hbm,
    index_hbm,
    out,
    level_base,
    level_slope,
    filter_table,
    filter_index,
    adj_u,
    adj_v,
    adj_zeta,
    depth,
    area,
    rho,
    um,
    vm,
    own_z,
    own_u,
    own_v,
    halo_z,
    halo_u,
    halo_v,
    static,
    halo_static,
    pack_west,
    pack_east,
    from_east,
    from_west,
    halo_east,
    halo_west,
    edge_z,
    edge_u,
    edge_v,
    edge_static,
    ring,
    edge_ring,
    own_state,
    edge_state,
    own_out,
    edge_out,
    own_halo,
    edge_halo,
    local_sem,
    bulk_send,
    bulk_recv,
    static_send,
    static_recv,
    lon_send,
    lon_recv,
    corner_send,
    corner_recv,
    state_send,
    state_recv,
):
    substeps, rows, columns = saved_z_hbm.shape
    levels = adj_u_hbm.shape[0]
    half = rows // 2
    blocks = substeps // SBLOCK
    lon = lax.axis_index("lon")
    lat = lax.axis_index("lat")
    east = lax.rem(lon + 1, lon_count)
    west = lax.rem(lon + lon_count - 1, lon_count)
    has_north = lat < lat_count - 1
    has_south = lat > 0
    saved_hbm = (saved_z_hbm, saved_u_hbm, saved_v_hbm)
    own = (own_z, own_u, own_v)
    halo = (halo_z, halo_u, halo_v)
    edge = (edge_z, edge_u, edge_v)
    state_outs = (own_out, edge_out)
    state_halos = (own_halo, edge_halo)

    small = (
        (adj_u_hbm, adj_u),
        (adj_v_hbm, adj_v),
        (adj_zeta_hbm, adj_zeta),
        (depth_hbm, depth),
        (area_hbm, area),
        (rho_hbm, rho),
        (um_hbm, um),
        (vm_hbm, vm),
        (base_hbm, level_base),
        (slope_hbm, level_slope),
        (table_hbm, filter_table),
        (index_hbm, filter_index),
    )
    small_copies = [
        pltpu.make_async_copy(src, dst, local_sem.at[i]) for i, (src, dst) in enumerate(small)
    ]
    split = substeps - SBLOCK
    saved_copies = []
    for part, (low, count) in enumerate(((split, SBLOCK), (0, split))):
        saved_copies.append(
            [
                pltpu.make_async_copy(
                    saved_hbm[f].at[pl.ds(low, count)],
                    own[f].at[pl.ds(low, count)],
                    local_sem.at[12 + 3 * part + f],
                )
                for f in range(3)
            ]
        )
    for copy in small_copies + saved_copies[0] + saved_copies[1]:
        copy.start()

    for there, at in ((has_north, pl.ds(0, half)), (has_south, pl.ds(half, half))):

        @pl.when(jnp.logical_not(there))
        def _():
            for target in (halo_z, halo_u, halo_v, halo_static, halo_east, halo_west):
                target[:, at, :] = jnp.zeros((target.shape[0], half, target.shape[2]), jnp.float32)
            for target in state_halos:
                target[:, :, at, :] = jnp.zeros(
                    target.shape[:2] + (half, target.shape[3]), jnp.float32
                )

    barrier = pltpu.get_barrier_semaphore()
    pl.semaphore_signal(barrier, inc=1, device_id={"lon": east}, device_id_type=MESH)
    pl.semaphore_signal(barrier, inc=1, device_id={"lon": west}, device_id_type=MESH)

    for there, row in ((has_north, lat + 1), (has_south, lat - 1)):

        @pl.when(there)
        def _():
            for column in (lon, east, west):
                pl.semaphore_signal(
                    barrier, inc=1, device_id={"lon": column, "lat": row}, device_id_type=MESH
                )

    pl.semaphore_wait(
        barrier, 2 + 3 * (jnp.minimum(lat, 1) + jnp.minimum(lat_count - 1 - lat, 1))
    )

    def lat_copy(src, dst, sends, recvs, northward, column=lon):
        return pltpu.make_async_remote_copy(
            src_ref=src,
            dst_ref=dst,
            send_sem=sends,
            recv_sem=recvs,
            device_id={"lon": column, "lat": lat + 1 if northward else lat - 1},
            device_id_type=MESH,
        )

    def bulk(block, northward):
        copies = []
        for inner in range(SBLOCK):
            reach = SBLOCK - inner
            n = substeps - 1 - block * SBLOCK - inner
            counts = (reach, reach - 1, reach - 1 if northward else reach)
            for f in range(3):
                if counts[f] == 0:
                    continue
                at = pl.ds(rows - counts[f] if northward else 0, counts[f])
                place = (int(northward), block, len(copies))
                copies.append(
                    lat_copy(
                        saved_hbm[f].at[n, at, :],
                        halo[f].at[n, at, :],
                        bulk_send.at[place],
                        bulk_recv.at[place],
                        northward,
                    )
                )
        return copies

    def halves(northward):
        return pl.ds(half, half) if northward else pl.ds(0, half)

    def static_copies(northward):
        at = halves(northward)
        return [
            lat_copy(
                static.at[:, at, :],
                halo_static.at[:, at, :],
                static_send.at[int(northward)],
                static_recv.at[int(northward)],
                northward,
            )
        ]

    groups = pack_west.shape[0]
    first = 2 + 3
    pieces = (pl.ds(0, first), pl.ds(first, groups - first))

    def lon_copies(part):
        at = pieces[part]
        return [
            pltpu.make_async_remote_copy(
                src_ref=src.at[at],
                dst_ref=dst.at[at],
                send_sem=lon_send.at[part, way],
                recv_sem=lon_recv.at[part, way],
                device_id={"lon": target},
                device_id_type=MESH,
            )
            for way, (src, dst, target) in enumerate(
                ((pack_west, from_east, west), (pack_east, from_west, east))
            )
        ]

    def corner_copies(part, northward):
        at = halves(northward)
        return [
            lat_copy(
                src.at[pieces[part], at, :],
                dst.at[pieces[part], at, :],
                corner_send.at[part, int(northward), way],
                corner_recv.at[part, int(northward), way],
                northward,
                target,
            )
            for way, (src, dst, target) in enumerate(
                ((pack_west, halo_east, west), (pack_east, halo_west, east))
            )
        ]

    def state_copies(chain, block, northward):
        at = halves(northward)
        return [
            lat_copy(
                state_outs[chain].at[block, :, at, :],
                state_halos[chain].at[block, :, at, :],
                state_send.at[chain, block, int(northward)],
                state_recv.at[chain, block, int(northward)],
                northward,
            )
        ]

    def start_lat(make):
        for northward, there in ((False, has_south), (True, has_north)):

            @pl.when(there)
            def _():
                for copy in make(northward):
                    copy.start()

    def wait_lat_recv(make):
        for northward, there in ((True, has_south), (False, has_north)):

            @pl.when(there)
            def _():
                for copy in make(northward):
                    copy.wait_recv()

    def wait_lat_send(make):
        for northward, there in ((False, has_south), (True, has_north)):

            @pl.when(there)
            def _():
                for copy in make(northward):
                    copy.wait_send()

    start_lat(functools.partial(bulk, 0))

    for copy in small_copies:
        copy.wait()

    def raw_weight(n):
        return filter_table[filter_index[n]]

    raw_sum = raw_weight(0)
    for n in range(1, substeps):
        raw_sum = raw_sum + raw_weight(n)
    inverse = 1.0 / jnp.full((rows, columns), raw_sum, jnp.float32)
    deep = depth[...]
    sum_u = jnp.sum(adj_u[...], axis=0)
    sum_v = jnp.sum(adj_v[...], axis=0)
    row_ids = lax.broadcasted_iota(jnp.int32, (rows, columns), 0)
    north_mask = jnp.where((row_ids == 0) & (lat == 0), 0.0, vm[...].astype(jnp.float32))
    cot_v = sum_v * inverse
    static[0] = deep
    static[1] = -flux_scale * rho[...].astype(jnp.float32) * area[...]
    static[2] = um[...].astype(jnp.float32)
    static[3] = north_mask
    static[4] = adj_zeta[...] * inverse
    static[5] = sum_u * inverse
    static[6] = cot_v

    def lacking(grad_north):
        ids = lax.broadcasted_iota(jnp.int32, grad_north.shape, 0)
        return jnp.where(ids == half - 1, slope_scale * north_of(grad_north), 0.0)

    static[7] = lacking(north_mask * (raw_weight(substeps - 1) * cot_v))
    start_lat(static_copies)

    quarter = lax.broadcasted_iota(jnp.int32, (rows, LANES), 1) // EDGE

    def pack(group, refs):
        to_west = rolled(refs[0][:, pl.ds(0, LANES)], 3 * EDGE, 1)
        to_east = rolled(refs[0][:, pl.ds(columns - LANES, LANES)], EDGE, 1)
        for q in range(1, 4):
            to_west = jnp.where(
                quarter == (q + 3) % 4,
                rolled(refs[q][:, pl.ds(0, LANES)], EDGE * (q + 3), 1),
                to_west,
            )
            to_east = jnp.where(
                quarter == q,
                rolled(refs[q][:, pl.ds(columns - LANES, LANES)], EDGE * (q + 1), 1),
                to_east,
            )
        pack_west[group] = to_west
        pack_east[group] = to_east

    def unpack(group, targets, sources, at, east_ref, west_ref):
        for q in range(4):
            both = jnp.where(quarter == q, west_ref[group], east_ref[group])
            both = rolled(both, -EDGE * q, 1)
            near_west = rolled(sources[q][:, pl.ds(0, LANES)], EDGE, 1)
            near_east = rolled(sources[q][:, pl.ds(columns - LANES, LANES)], -EDGE, 1)
            targets[q][at, pl.ds(0, LANES)] = jnp.where(quarter == 0, both, near_west)
            targets[q][at, pl.ds(LANES, LANES)] = jnp.where(quarter == 3, both, near_east)

    top, bottom = pl.ds(0, rows), pl.ds(rows, rows)
    sides = ((own, static, top, from_east, from_west),)
    sides += ((halo, halo_static, bottom, halo_east, halo_west),)

    def block_fields(block, refs):
        top = substeps - 1 - block * SBLOCK
        return [refs[k % 3].at[top - k // 3] for k in range(3 * SBLOCK)]

    def pack_block(block):
        fields = block_fields(block, own)
        for g in range(3):
            pack(2 + 3 * block + g, fields[4 * g : 4 * g + 4])

    def unpack_block(block):
        targets = block_fields(block, edge)
        for refs, _, at, east_ref, west_ref in sides:
            sources = block_fields(block, refs)
            for g in range(3):
                some = slice(4 * g, 4 * g + 4)
                unpack(2 + 3 * block + g, targets[some], sources[some], at, east_ref, west_ref)

    for g in range(2):
        pack(g, [static.at[4 * g + q] for q in range(4)])
    for copy in saved_copies[0]:
        copy.wait()
    pack_block(0)
    for copy in lon_copies(0):
        copy.start()
    start_lat(functools.partial(corner_copies, 0))
    for copy in saved_copies[1]:
        copy.wait()

    def pack_turn(block, carry):
        pack_block(block)
        return carry

    lax.fori_loop(1, blocks, pack_turn, 0)
    for copy in lon_copies(1):
        copy.start()
    start_lat(functools.partial(corner_copies, 1))
    start_lat(functools.partial(bulk, 1))

    total = level_base[0] + level_slope[0] * deep
    for k in range(1, levels):
        total = total + (level_base[k] + level_slope[k] * deep)
    share_u = sum_u / total
    share_v = sum_v / total
    for k in range(levels):
        thick = level_base[k] + level_slope[k] * deep
        out[3 + k] = adj_u[k] - thick * share_u
        out[3 + levels + k] = adj_v[k] - thick * share_v

    def both(own_ref, halo_ref, index):
        return jnp.concatenate([own_ref[index], halo_ref[index]], axis=0)

    def no_seam(values):
        ids = lax.broadcasted_iota(jnp.int32, values.shape, 0)
        return jnp.where(ids == rows + half - 1, 0.0, values)

    def start_chain(ring_ref, fields):
        deep, area_factor, east_mask, north_mask, cot_z, cot_u, cot_v = fields
        ring_ref[0] = east_mask * (0.5 * (deep + west_of(deep)))
        ring_ref[1] = north_mask * (0.5 * (deep + south_of(deep)))
        ring_ref[2] = area_factor
        ring_ref[3] = 0.5 * east_mask
        ring_ref[4] = 0.5 * north_mask
        cot_east, cot_north = east_mask * cot_u, north_mask * cot_v
        next_east, next_north = east_of(cot_east), no_seam(north_of(cot_north))
        ring_ref[5] = cot_z - slope_scale * (cot_east - next_east + cot_north - next_north)
        ring_ref[6] = cot_east
        ring_ref[7] = cot_north
        ring_ref[8] = next_east
        ring_ref[9] = next_north

    def start_state(state_ref, missing):
        for k in range(5):
            state_ref[k] = jnp.zeros(state_ref.shape[1:], jnp.float32)
        state_ref[0, bottom, :] = missing

    def substep(n, ring_ref, state_ref, saved_z, saved_u, saved_v):
        weight = raw_weight(n)
        east_depth = ring_ref[0] + ring_ref[3] * (saved_z + west_of(saved_z))
        north_depth = ring_ref[1] + ring_ref[4] * (saved_z + south_of(saved_z))
        east_speed = ring_ref[3] * saved_u
        north_speed = ring_ref[4] * saved_v
        u, v, next_u, next_v = state_ref[1], state_ref[2], state_ref[3], state_ref[4]
        zeta_total = (state_ref[0] + weight * ring_ref[5]) - slope_scale * (
            (u - next_u) + (v - next_v)
        )
        flux = ring_ref[2] * zeta_total
        west_pull = west_of(flux) - flux
        east_pull = flux - east_of(flux)
        south_pull = south_of(flux) - flux
        north_pull = flux - north_of(flux)
        state_ref[0] = (
            zeta_total
            + (east_speed * west_pull + east_of(east_speed) * east_pull)
            + (north_speed * south_pull + north_of(north_speed) * north_pull)
        )
        state_ref[1] = keep_rate * (u + weight * ring_ref[6]) + east_depth * west_pull
        state_ref[2] = keep_rate * (v + weight * ring_ref[7]) + north_depth * south_pull
        state_ref[3] = (
            keep_rate * (next_u + weight * ring_ref[8]) + east_of(east_depth) * east_pull
        )
        state_ref[4] = (
            keep_rate * (next_v + weight * ring_ref[9]) + north_of(north_depth) * north_pull
        )

    chains = ((ring, own_state), (edge_ring, edge_state))

    def run_block(chain, block):
        ring_ref, state_ref = chains[chain]
        if block > 0:
            wait_lat_recv(functools.partial(state_copies, chain, block - 1))
            for k in range(3):
                state_ref[k, bottom, :] = state_halos[chain][block - 1, k]
            state_ref[3] = east_of(state_ref[1])
            state_ref[4] = no_seam(north_of(state_ref[2]))

        def turn(inner, carry):
            n = substeps - 1 - block * SBLOCK - inner
            if chain == 0:
                saved = [both(own[f], halo[f], n) for f in range(3)]
            else:
                saved = [edge[f][n] for f in range(3)]
            substep(n, ring_ref, state_ref, *saved)
            return carry

        lax.fori_loop(0, SBLOCK, turn, 0, unroll=True)
        if block < blocks - 1:
            out_ref = state_outs[chain]
            weight = raw_weight(substeps - 1 - (block + 1) * SBLOCK)
            missing = slope_scale * (state_ref[4, top, :] + weight * ring_ref[9, top, :])
            ids = lax.broadcasted_iota(jnp.int32, missing.shape, 0)
            out_ref[block, 0] = state_ref[0, top, :] + jnp.where(ids == half - 1, missing, 0.0)
            out_ref[block, 1] = state_ref[1, top, :]
            out_ref[block, 2] = state_ref[2, top, :]
            start_lat(functools.partial(state_copies, chain, block))

    wait_lat_recv(static_copies)
    start_chain(ring, [both(static, halo_static, k) for k in range(7)])
    start_state(own_state, halo_static[7])
    for block in range(blocks):
        wait_lat_recv(functools.partial(bulk, block))
        run_block(0, block)
        if block < 2:
            for copy in lon_copies(block):
                copy.wait_recv()
            wait_lat_recv(functools.partial(corner_copies, block))
        if block == 0:
            for _, refs, at, east_ref, west_ref in sides:
                for g in range(2):
                    some = range(4 * g, 4 * g + 4)
                    unpack(
                        g,
                        [edge_static.at[k] for k in some],
                        [refs.at[k] for k in some],
                        at,
                        east_ref,
                        west_ref,
                    )
            start_chain(edge_ring, [edge_static[k] for k in range(7)])
            start_state(edge_state, edge_static[7, bottom, :])
        unpack_block(block)
        run_block(1, block)
        if block + 2 < blocks:
            start_lat(functools.partial(bulk, block + 2))

    lane = lax.broadcasted_iota(jnp.int32, (rows, LANES), 1)
    last = columns - LANES
    for k in range(3):
        out[k] = own_state[k, top, :]
        out[k, :, pl.ds(0, LANES)] = jnp.where(
            lane < EDGE,
            rolled(edge_state[k, top, pl.ds(0, LANES)], -EDGE, 1),
            own_state[k, top, pl.ds(0, LANES)],
        )
        out[k, :, pl.ds(last, LANES)] = jnp.where(
            lane >= LANES - EDGE,
            rolled(edge_state[k, top, pl.ds(LANES, LANES)], EDGE, 1),
            own_state[k, top, pl.ds(last, LANES)],
        )

    for part in range(2):
        for copy in lon_copies(part):
            copy.wait_send()
        wait_lat_send(functools.partial(corner_copies, part))
    wait_lat_send(static_copies)
    for block in range(blocks):
        wait_lat_send(functools.partial(bulk, block))
        if block < blocks - 1:
            for chain in range(2):
                wait_lat_send(functools.partial(state_copies, chain, block))


def hand_out(together, out_z, out_u, out_v, out_u3, out_v3, held, sems):
    levels = out_u3.shape[0]
    places = (pl.ds(3, levels), pl.ds(3 + levels, levels), 0, 1, 2)
    outs = (out_u3, out_v3, out_z, out_u, out_v)
    ins = [
        pltpu.make_async_copy(together.at[at], held.at[at], sems.at[0, i])
        for i, at in enumerate(places)
    ]
    copies = [
        pltpu.make_async_copy(held.at[at], out, sems.at[1, i])
        for i, (at, out) in enumerate(zip(places, outs))
    ]
    for copy in ins:
        copy.start()
    for arrival, copy in zip(ins, copies):
        arrival.wait()
        copy.start()
    for copy in copies:
        copy.wait()


def body(
    lon_count,
    lat_count,
    adj_u,
    adj_v,
    adj_zeta,
    saved_zeta,
    saved_ubar,
    stored_mean_north_velocity,
    depth,
    scaled_inverse_area,
    level_base,
    level_slope,
    rho_mask,
    u_mask,
    v_mask,
    filter_table,
    filter_index,
):
    rows, columns = depth.shape
    substeps = saved_zeta.shape[0]
    levels = adj_u.shape[0]
    blocks = substeps // SBLOCK
    spans = (columns, 2 * LANES)
    groups = 2 + 3 * blocks
    most = 3 * SBLOCK
    f32, i32 = jnp.float32, jnp.int32
    flat = jax.ShapeDtypeStruct((rows, columns), f32)
    tall = jax.ShapeDtypeStruct((levels, rows, columns), f32)
    saved = pltpu.VMEM((substeps, rows, columns), f32)
    packed = pltpu.VMEM((groups, rows, LANES), f32)
    dma = pltpu.SemaphoreType.DMA
    hbm = pl.BlockSpec(memory_space=pltpu.HBM)
    together = pl.pallas_call(
        functools.partial(kernel, lon_count, lat_count),
        out_shape=jax.ShapeDtypeStruct((3 + 2 * levels, rows, columns), f32),
        in_specs=[hbm] * 15,
        out_specs=pl.BlockSpec(memory_space=pltpu.VMEM),
        scratch_shapes=[
            pltpu.SMEM((levels,), f32),
            pltpu.SMEM((levels,), f32),
            pltpu.SMEM(filter_table.shape, f32),
            pltpu.SMEM(filter_index.shape, i32),
            pltpu.VMEM((levels, rows, columns), f32),
            pltpu.VMEM((levels, rows, columns), f32),
            pltpu.VMEM((rows, columns), f32),
            pltpu.VMEM((rows, columns), f32),
            pltpu.VMEM((rows, columns), f32),
            pltpu.VMEM((rows, columns), i32),
            pltpu.VMEM((rows, columns), i32),
            pltpu.VMEM((rows, columns), i32),
            saved,
            saved,
            saved,
            saved,
            saved,
            saved,
            pltpu.VMEM((8, rows, columns), f32),
            pltpu.VMEM((8, rows, columns), f32),
            packed,
            packed,
            packed,
            packed,
            packed,
            packed,
            pltpu.VMEM((substeps, 2 * rows, 2 * LANES), f32),
            pltpu.VMEM((substeps, 2 * rows, 2 * LANES), f32),
            pltpu.VMEM((substeps, 2 * rows, 2 * LANES), f32),
            pltpu.VMEM((8, 2 * rows, 2 * LANES), f32),
            pltpu.VMEM((10, 2 * rows, columns), f32),
            pltpu.VMEM((10, 2 * rows, 2 * LANES), f32),
            *[pltpu.VMEM((5, 2 * rows, span), f32) for span in spans],
            *[pltpu.VMEM((blocks - 1, 3, rows, span), f32) for span in spans * 2],
            dma((18,)),
            dma((2, blocks, most)),
            dma((2, blocks, most)),
            dma((2,)),
            dma((2,)),
            dma((2, 2)),
            dma((2, 2)),
            dma((2, 2, 2)),
            dma((2, 2, 2)),
            dma((2, blocks - 1, 2)),
            dma((2, blocks - 1, 2)),
        ],
        compiler_params=pltpu.CompilerParams(
            collective_id=0, has_side_effects=True, vmem_limit_bytes=56 * 1024 * 1024
        ),
    )(
        adj_u,
        adj_v,
        adj_zeta,
        saved_zeta,
        saved_ubar,
        stored_mean_north_velocity,
        depth,
        scaled_inverse_area,
        rho_mask,
        u_mask,
        v_mask,
        level_base,
        level_slope,
        filter_table,
        filter_index,
    )
    return pl.pallas_call(
        hand_out,
        out_shape=(flat, flat, flat, tall, tall),
        in_specs=[hbm],
        out_specs=(hbm,) * 5,
        scratch_shapes=[pltpu.VMEM((3 + 2 * levels, rows, columns), f32), dma((2, 5))],
    )(together)


def solution(mesh):
    placed = (
        P(None, "lat", "lon"),
        P(None, "lat", "lon"),
        P("lat", "lon"),
        P(None, "lat", "lon"),
        P(None, "lat", "lon"),
        P(None, "lat", "lon"),
        P("lat", "lon"),
        P("lat", "lon"),
        P(),
        P(),
        P("lat", "lon"),
        P("lat", "lon"),
        P("lat", "lon"),
        P(),
        P(),
    )
    return jax.shard_map(
        functools.partial(body, mesh.shape["lon"], mesh.shape["lat"]),
        mesh=mesh,
        in_specs=placed,
        out_specs=(
            P("lat", "lon"),
            P("lat", "lon"),
            P("lat", "lon"),
            P(None, "lat", "lon"),
            P(None, "lat", "lon"),
        ),
        check_vma=False,
    )
```

```python
import functools

import jax
import jax.numpy as jnp
from jax import lax
from jax.experimental import pallas as pl
from jax.experimental.pallas import tpu as pltpu
from jax.sharding import PartitionSpec as P

SBLOCK = 4
EDGE = 32
LANES = 128

flux_scale = 0.3
slope_scale = 0.3
keep_rate = 0.98
MESH = pl.DeviceIdType.MESH


def rolled(values, shift, axis):
    return pltpu.roll(values, shift % values.shape[axis], axis)


def east_of(values):
    return rolled(values, -1, 1)


def west_of(values):
    return rolled(values, 1, 1)


def north_of(values):
    return rolled(values, -1, 0)


def south_of(values):
    return rolled(values, 1, 0)


def kernel(
    lon_count,
    lat_count,
    adj_u_hbm,
    adj_v_hbm,
    adj_zeta_hbm,
    saved_z_hbm,
    saved_u_hbm,
    saved_v_hbm,
    depth_hbm,
    area_hbm,
    rho_hbm,
    um_hbm,
    vm_hbm,
    base_hbm,
    slope_hbm,
    table_hbm,
    index_hbm,
    out,
    level_base,
    level_slope,
    filter_table,
    filter_index,
    adj_u,
    adj_v,
    adj_zeta,
    depth,
    area,
    rho,
    um,
    vm,
    own_z,
    own_u,
    own_v,
    halo_z,
    halo_u,
    halo_v,
    static,
    halo_static,
    pack_west,
    pack_east,
    from_east,
    from_west,
    halo_east,
    halo_west,
    edge_z,
    edge_u,
    edge_v,
    edge_static,
    ring,
    edge_ring,
    ahead,
    own_state,
    edge_state,
    own_out,
    edge_out,
    own_halo,
    edge_halo,
    local_sem,
    bulk_send,
    bulk_recv,
    static_send,
    static_recv,
    lon_send,
    lon_recv,
    corner_send,
    corner_recv,
    state_send,
    state_recv,
):
    substeps, rows, columns = saved_z_hbm.shape
    levels = adj_u_hbm.shape[0]
    half = rows // 2
    blocks = substeps // SBLOCK
    lon = lax.axis_index("lon")
    lat = lax.axis_index("lat")
    east = lax.rem(lon + 1, lon_count)
    west = lax.rem(lon + lon_count - 1, lon_count)
    has_north = lat < lat_count - 1
    has_south = lat > 0
    saved_hbm = (saved_z_hbm, saved_u_hbm, saved_v_hbm)
    own = (own_z, own_u, own_v)
    halo = (halo_z, halo_u, halo_v)
    edge = (edge_z, edge_u, edge_v)
    state_outs = (own_out, edge_out)
    state_halos = (own_halo, edge_halo)

    barrier = pltpu.get_barrier_semaphore()
    pl.semaphore_signal(barrier, inc=1, device_id={"lon": east}, device_id_type=MESH)
    pl.semaphore_signal(barrier, inc=1, device_id={"lon": west}, device_id_type=MESH)

    for there, row in ((has_north, lat + 1), (has_south, lat - 1)):

        @pl.when(there)
        def _():
            for column in (lon, east, west):
                pl.semaphore_signal(
                    barrier, inc=1, device_id={"lon": column, "lat": row}, device_id_type=MESH
                )

    small = (
        (adj_u_hbm, adj_u),
        (adj_v_hbm, adj_v),
        (adj_zeta_hbm, adj_zeta),
        (depth_hbm, depth),
        (area_hbm, area),
        (rho_hbm, rho),
        (um_hbm, um),
        (vm_hbm, vm),
        (base_hbm, level_base),
        (slope_hbm, level_slope),
        (table_hbm, filter_table),
        (index_hbm, filter_index),
    )
    small_copies = [
        pltpu.make_async_copy(src, dst, local_sem.at[i]) for i, (src, dst) in enumerate(small)
    ]
    split = substeps - SBLOCK
    saved_copies = []
    for part, (low, count) in enumerate(((split, SBLOCK), (0, split))):
        saved_copies.append(
            [
                pltpu.make_async_copy(
                    saved_hbm[f].at[pl.ds(low, count)],
                    own[f].at[pl.ds(low, count)],
                    local_sem.at[12 + 3 * part + f],
                )
                for f in range(3)
            ]
        )
    for copy in small_copies + saved_copies[0] + saved_copies[1]:
        copy.start()

    pl.semaphore_wait(
        barrier, 2 + 3 * (jnp.minimum(lat, 1) + jnp.minimum(lat_count - 1 - lat, 1))
    )

    def lat_copy(src, dst, sends, recvs, northward, column=lon):
        return pltpu.make_async_remote_copy(
            src_ref=src,
            dst_ref=dst,
            send_sem=sends,
            recv_sem=recvs,
            device_id={"lon": column, "lat": lat + 1 if northward else lat - 1},
            device_id_type=MESH,
        )

    def bulk(block, northward):
        copies = []
        for inner in range(SBLOCK):
            reach = SBLOCK - inner
            n = substeps - 1 - block * SBLOCK - inner
            counts = (reach, reach - 1, reach - 1 if northward else reach)
            for f in range(3):
                if counts[f] == 0:
                    continue
                at = pl.ds(rows - counts[f] if northward else 0, counts[f])
                place = (int(northward), block, len(copies))
                copies.append(
                    lat_copy(
                        saved_hbm[f].at[n, at, :],
                        halo[f].at[n, at, :],
                        bulk_send.at[place],
                        bulk_recv.at[place],
                        northward,
                    )
                )
        return copies

    def halves(northward):
        return pl.ds(half, half) if northward else pl.ds(0, half)

    def static_copies(northward):
        at = halves(northward)
        return [
            lat_copy(
                static.at[:, at, :],
                halo_static.at[:, at, :],
                static_send.at[int(northward)],
                static_recv.at[int(northward)],
                northward,
            )
        ]

    groups = pack_west.shape[0]
    first = 2 + 3
    pieces = (pl.ds(0, first), pl.ds(first, groups - first))

    def lon_copies(part):
        at = pieces[part]
        return [
            pltpu.make_async_remote_copy(
                src_ref=src.at[at],
                dst_ref=dst.at[at],
                send_sem=lon_send.at[part, way],
                recv_sem=lon_recv.at[part, way],
                device_id={"lon": target},
                device_id_type=MESH,
            )
            for way, (src, dst, target) in enumerate(
                ((pack_west, from_east, west), (pack_east, from_west, east))
            )
        ]

    def corner_copies(part, northward):
        at = halves(northward)
        return [
            lat_copy(
                src.at[pieces[part], at, :],
                dst.at[pieces[part], at, :],
                corner_send.at[part, int(northward), way],
                corner_recv.at[part, int(northward), way],
                northward,
                target,
            )
            for way, (src, dst, target) in enumerate(
                ((pack_west, halo_east, west), (pack_east, halo_west, east))
            )
        ]

    def state_copies(chain, block, northward):
        at = halves(northward)
        return [
            lat_copy(
                state_outs[chain].at[block, :, at, :],
                state_halos[chain].at[block, :, at, :],
                state_send.at[chain, block, int(northward)],
                state_recv.at[chain, block, int(northward)],
                northward,
            )
        ]

    def start_lat(make):
        for northward, there in ((False, has_south), (True, has_north)):

            @pl.when(there)
            def _():
                for copy in make(northward):
                    copy.start()

    def wait_lat_recv(make):
        for northward, there in ((True, has_south), (False, has_north)):

            @pl.when(there)
            def _():
                for copy in make(northward):
                    copy.wait_recv()

    def wait_lat_send(make):
        for northward, there in ((False, has_south), (True, has_north)):

            @pl.when(there)
            def _():
                for copy in make(northward):
                    copy.wait_send()

    start_lat(functools.partial(bulk, 0))

    for there, at in ((has_north, pl.ds(0, half)), (has_south, pl.ds(half, half))):

        @pl.when(jnp.logical_not(there))
        def _():
            for target in (halo_z, halo_u, halo_v, halo_static, halo_east, halo_west):
                target[:, at, :] = jnp.zeros((target.shape[0], half, target.shape[2]), jnp.float32)
            for target in state_halos:
                target[:, :, at, :] = jnp.zeros(
                    target.shape[:2] + (half, target.shape[3]), jnp.float32
                )

    for copy in small_copies:
        copy.wait()

    def raw_weight(n):
        return filter_table[filter_index[n]]

    raw_sum = raw_weight(0)
    for n in range(1, substeps):
        raw_sum = raw_sum + raw_weight(n)
    inverse = 1.0 / jnp.full((rows, columns), raw_sum, jnp.float32)
    deep = depth[...]
    sum_u = jnp.sum(adj_u[...], axis=0)
    sum_v = jnp.sum(adj_v[...], axis=0)
    row_ids = lax.broadcasted_iota(jnp.int32, (rows, columns), 0)
    north_mask = jnp.where((row_ids == 0) & (lat == 0), 0.0, vm[...].astype(jnp.float32))
    cot_v = sum_v * inverse
    static[0] = deep
    static[1] = -flux_scale * rho[...].astype(jnp.float32) * area[...]
    static[2] = um[...].astype(jnp.float32)
    static[3] = north_mask
    static[4] = adj_zeta[...] * inverse
    static[5] = sum_u * inverse
    static[6] = cot_v

    def lacking(grad_north):
        ids = lax.broadcasted_iota(jnp.int32, grad_north.shape, 0)
        return jnp.where(ids == half - 1, slope_scale * north_of(grad_north), 0.0)

    static[7] = lacking(north_mask * (raw_weight(substeps - 1) * cot_v))
    start_lat(static_copies)

    quarter = lax.broadcasted_iota(jnp.int32, (rows, LANES), 1) // EDGE

    def pack(group, refs):
        to_west = rolled(refs[0][:, pl.ds(0, LANES)], 3 * EDGE, 1)
        to_east = rolled(refs[0][:, pl.ds(columns - LANES, LANES)], EDGE, 1)
        for q in range(1, 4):
            to_west = jnp.where(
                quarter == (q + 3) % 4,
                rolled(refs[q][:, pl.ds(0, LANES)], EDGE * (q + 3), 1),
                to_west,
            )
            to_east = jnp.where(
                quarter == q,
                rolled(refs[q][:, pl.ds(columns - LANES, LANES)], EDGE * (q + 1), 1),
                to_east,
            )
        pack_west[group] = to_west
        pack_east[group] = to_east

    def unpack(group, targets, sources, at, east_ref, west_ref):
        for q in range(4):
            both = jnp.where(quarter == q, west_ref[group], east_ref[group])
            both = rolled(both, -EDGE * q, 1)
            near_west = rolled(sources[q][:, pl.ds(0, LANES)], EDGE, 1)
            near_east = rolled(sources[q][:, pl.ds(columns - LANES, LANES)], -EDGE, 1)
            targets[q][at, pl.ds(0, LANES)] = jnp.where(quarter == 0, both, near_west)
            targets[q][at, pl.ds(LANES, LANES)] = jnp.where(quarter == 3, both, near_east)

    top, bottom = pl.ds(0, rows), pl.ds(rows, rows)
    sides = ((own, static, top, from_east, from_west),)
    sides += ((halo, halo_static, bottom, halo_east, halo_west),)

    def block_fields(block, refs):
        top = substeps - 1 - block * SBLOCK
        return [refs[k % 3].at[top - k // 3] for k in range(3 * SBLOCK)]

    def pack_block(block):
        fields = block_fields(block, own)
        for g in range(3):
            pack(2 + 3 * block + g, fields[4 * g : 4 * g + 4])

    def unpack_block(block):
        targets = block_fields(block, edge)
        for refs, _, at, east_ref, west_ref in sides:
            sources = block_fields(block, refs)
            for g in range(3):
                some = slice(4 * g, 4 * g + 4)
                unpack(2 + 3 * block + g, targets[some], sources[some], at, east_ref, west_ref)

    for g in range(2):
        pack(g, [static.at[4 * g + q] for q in range(4)])
    for copy in saved_copies[0]:
        copy.wait()
    pack_block(0)
    for copy in lon_copies(0):
        copy.start()
    start_lat(functools.partial(corner_copies, 0))
    for copy in saved_copies[1]:
        copy.wait()

    def pack_turn(block, carry):
        pack_block(block)
        return carry

    lax.fori_loop(1, blocks, pack_turn, 0)
    for copy in lon_copies(1):
        copy.start()
    start_lat(functools.partial(corner_copies, 1))
    start_lat(functools.partial(bulk, 1))

    total = level_base[0] + level_slope[0] * deep
    for k in range(1, levels):
        total = total + (level_base[k] + level_slope[k] * deep)
    share_u = sum_u / total
    share_v = sum_v / total
    for k in range(levels):
        thick = level_base[k] + level_slope[k] * deep
        out[3 + k] = adj_u[k] - thick * share_u
        out[3 + levels + k] = adj_v[k] - thick * share_v

    def both(own_ref, halo_ref, index):
        return jnp.concatenate([own_ref[index], halo_ref[index]], axis=0)

    def no_seam(values):
        ids = lax.broadcasted_iota(jnp.int32, values.shape, 0)
        return jnp.where(ids == rows + half - 1, 0.0, values)

    def start_chain(ring_ref, fields):
        deep, area_factor, east_mask, north_mask, cot_z, cot_u, cot_v = fields
        ring_ref[0] = east_mask * (0.5 * (deep + west_of(deep)))
        ring_ref[1] = north_mask * (0.5 * (deep + south_of(deep)))
        ring_ref[2] = area_factor
        ring_ref[3] = 0.5 * east_mask
        ring_ref[4] = 0.5 * north_mask
        cot_east, cot_north = east_mask * cot_u, north_mask * cot_v
        next_east, next_north = east_of(cot_east), no_seam(north_of(cot_north))
        ring_ref[5] = cot_z - slope_scale * (cot_east - next_east + cot_north - next_north)
        ring_ref[6] = cot_east
        ring_ref[7] = cot_north
        ring_ref[8] = next_east
        ring_ref[9] = next_north

    def start_state(state_ref, missing):
        for k in range(5):
            state_ref[k] = jnp.zeros(state_ref.shape[1:], jnp.float32)
        state_ref[0, bottom, :] = missing

    def factors_of(ring_ref, saved_z, saved_u, saved_v):
        east_depth = ring_ref[0] + ring_ref[3] * (saved_z + west_of(saved_z))
        north_depth = ring_ref[1] + ring_ref[4] * (saved_z + south_of(saved_z))
        east_speed = ring_ref[3] * saved_u
        north_speed = ring_ref[4] * saved_v
        return (
            east_depth,
            north_depth,
            east_of(east_depth),
            north_of(north_depth),
            east_speed,
            north_speed,
            east_of(east_speed),
            north_of(north_speed),
        )

    def prepare(block):
        wait_lat_recv(functools.partial(bulk, block))
        for inner in range(SBLOCK):
            n = substeps - 1 - block * SBLOCK - inner
            for k, factor in enumerate(factors_of(ring, *(both(own[f], halo[f], n) for f in range(3)))):
                ahead[inner, k] = factor

    def substep(n, ring_ref, state_ref, factors):
        weight = raw_weight(n)
        east_depth, north_depth, next_depth, far_depth = factors[:4]
        east_speed, north_speed, next_speed, far_speed = factors[4:]
        u, v, next_u, next_v = state_ref[1], state_ref[2], state_ref[3], state_ref[4]
        zeta_total = (state_ref[0] + weight * ring_ref[5]) - slope_scale * (
            (u - next_u) + (v - next_v)
        )
        flux = ring_ref[2] * zeta_total
        west_pull = west_of(flux) - flux
        east_pull = flux - east_of(flux)
        south_pull = south_of(flux) - flux
        north_pull = flux - north_of(flux)
        state_ref[0] = (
            zeta_total
            + (east_speed * west_pull + next_speed * east_pull)
            + (north_speed * south_pull + far_speed * north_pull)
        )
        state_ref[1] = keep_rate * (u + weight * ring_ref[6]) + east_depth * west_pull
        state_ref[2] = keep_rate * (v + weight * ring_ref[7]) + north_depth * south_pull
        state_ref[3] = (
            keep_rate * (next_u + weight * ring_ref[8]) + next_depth * east_pull
        )
        state_ref[4] = (
            keep_rate * (next_v + weight * ring_ref[9]) + far_depth * north_pull
        )

    chains = ((ring, own_state), (edge_ring, edge_state))

    def run_block(chain, block):
        ring_ref, state_ref = chains[chain]
        if block > 0:
            wait_lat_recv(functools.partial(state_copies, chain, block - 1))
            for k in range(3):
                state_ref[k, bottom, :] = state_halos[chain][block - 1, k]
            state_ref[3] = east_of(state_ref[1])
            state_ref[4] = no_seam(north_of(state_ref[2]))

        def turn(inner, carry):
            n = substeps - 1 - block * SBLOCK - inner
            if chain == 0:
                factors = [ahead[inner, k] for k in range(8)]
            else:
                factors = factors_of(ring_ref, *(edge[f][n] for f in range(3)))
            substep(n, ring_ref, state_ref, factors)
            return carry

        lax.fori_loop(0, SBLOCK, turn, 0, unroll=True)
        if block < blocks - 1:
            out_ref = state_outs[chain]
            weight = raw_weight(substeps - 1 - (block + 1) * SBLOCK)
            missing = slope_scale * (state_ref[4, top, :] + weight * ring_ref[9, top, :])
            ids = lax.broadcasted_iota(jnp.int32, missing.shape, 0)
            out_ref[block, 0] = state_ref[0, top, :] + jnp.where(ids == half - 1, missing, 0.0)
            out_ref[block, 1] = state_ref[1, top, :]
            out_ref[block, 2] = state_ref[2, top, :]
            start_lat(functools.partial(state_copies, chain, block))

    wait_lat_recv(static_copies)
    start_chain(ring, [both(static, halo_static, k) for k in range(7)])
    start_state(own_state, halo_static[7])
    prepare(0)
    for block in range(blocks):
        run_block(0, block)
        if block < 2:
            for copy in lon_copies(block):
                copy.wait_recv()
            wait_lat_recv(functools.partial(corner_copies, block))
        if block == 0:
            for _, refs, at, east_ref, west_ref in sides:
                for g in range(2):
                    some = range(4 * g, 4 * g + 4)
                    unpack(
                        g,
                        [edge_static.at[k] for k in some],
                        [refs.at[k] for k in some],
                        at,
                        east_ref,
                        west_ref,
                    )
            start_chain(edge_ring, [edge_static[k] for k in range(7)])
            start_state(edge_state, edge_static[7, bottom, :])
        unpack_block(block)
        run_block(1, block)
        if block + 2 < blocks:
            start_lat(functools.partial(bulk, block + 2))
        if block + 1 < blocks:
            prepare(block + 1)

    lane = lax.broadcasted_iota(jnp.int32, (rows, LANES), 1)
    last = columns - LANES
    for k in range(3):
        out[k] = own_state[k, top, :]
        out[k, :, pl.ds(0, LANES)] = jnp.where(
            lane < EDGE,
            rolled(edge_state[k, top, pl.ds(0, LANES)], -EDGE, 1),
            own_state[k, top, pl.ds(0, LANES)],
        )
        out[k, :, pl.ds(last, LANES)] = jnp.where(
            lane >= LANES - EDGE,
            rolled(edge_state[k, top, pl.ds(LANES, LANES)], EDGE, 1),
            own_state[k, top, pl.ds(last, LANES)],
        )

    for part in range(2):
        for copy in lon_copies(part):
            copy.wait_send()
        wait_lat_send(functools.partial(corner_copies, part))
    wait_lat_send(static_copies)
    for block in range(blocks):
        wait_lat_send(functools.partial(bulk, block))
        if block < blocks - 1:
            for chain in range(2):
                wait_lat_send(functools.partial(state_copies, chain, block))


def hand_out(together, out_z, out_u, out_v, out_u3, out_v3, held, sems):
    levels = out_u3.shape[0]
    places = (pl.ds(3, levels), pl.ds(3 + levels, levels), 0, 1, 2)
    outs = (out_u3, out_v3, out_z, out_u, out_v)
    ins = [
        pltpu.make_async_copy(together.at[at], held.at[at], sems.at[0, i])
        for i, at in enumerate(places)
    ]
    copies = [
        pltpu.make_async_copy(held.at[at], out, sems.at[1, i])
        for i, (at, out) in enumerate(zip(places, outs))
    ]
    for copy in ins:
        copy.start()
    for arrival, copy in zip(ins, copies):
        arrival.wait()
        copy.start()
    for copy in copies:
        copy.wait()


def body(
    lon_count,
    lat_count,
    adj_u,
    adj_v,
    adj_zeta,
    saved_zeta,
    saved_ubar,
    stored_mean_north_velocity,
    depth,
    scaled_inverse_area,
    level_base,
    level_slope,
    rho_mask,
    u_mask,
    v_mask,
    filter_table,
    filter_index,
):
    rows, columns = depth.shape
    substeps = saved_zeta.shape[0]
    levels = adj_u.shape[0]
    blocks = substeps // SBLOCK
    spans = (columns, 2 * LANES)
    groups = 2 + 3 * blocks
    most = 3 * SBLOCK
    f32, i32 = jnp.float32, jnp.int32
    flat = jax.ShapeDtypeStruct((rows, columns), f32)
    tall = jax.ShapeDtypeStruct((levels, rows, columns), f32)
    saved = pltpu.VMEM((substeps, rows, columns), f32)
    packed = pltpu.VMEM((groups, rows, LANES), f32)
    dma = pltpu.SemaphoreType.DMA
    hbm = pl.BlockSpec(memory_space=pltpu.HBM)
    together = pl.pallas_call(
        functools.partial(kernel, lon_count, lat_count),
        out_shape=jax.ShapeDtypeStruct((3 + 2 * levels, rows, columns), f32),
        in_specs=[hbm] * 15,
        out_specs=pl.BlockSpec(memory_space=pltpu.VMEM),
        scratch_shapes=[
            pltpu.SMEM((levels,), f32),
            pltpu.SMEM((levels,), f32),
            pltpu.SMEM(filter_table.shape, f32),
            pltpu.SMEM(filter_index.shape, i32),
            pltpu.VMEM((levels, rows, columns), f32),
            pltpu.VMEM((levels, rows, columns), f32),
            pltpu.VMEM((rows, columns), f32),
            pltpu.VMEM((rows, columns), f32),
            pltpu.VMEM((rows, columns), f32),
            pltpu.VMEM((rows, columns), i32),
            pltpu.VMEM((rows, columns), i32),
            pltpu.VMEM((rows, columns), i32),
            saved,
            saved,
            saved,
            saved,
            saved,
            saved,
            pltpu.VMEM((8, rows, columns), f32),
            pltpu.VMEM((8, rows, columns), f32),
            packed,
            packed,
            packed,
            packed,
            packed,
            packed,
            pltpu.VMEM((substeps, 2 * rows, 2 * LANES), f32),
            pltpu.VMEM((substeps, 2 * rows, 2 * LANES), f32),
            pltpu.VMEM((substeps, 2 * rows, 2 * LANES), f32),
            pltpu.VMEM((8, 2 * rows, 2 * LANES), f32),
            pltpu.VMEM((10, 2 * rows, columns), f32),
            pltpu.VMEM((10, 2 * rows, 2 * LANES), f32),
            pltpu.VMEM((SBLOCK, 8, 2 * rows, columns), f32),
            *[pltpu.VMEM((5, 2 * rows, span), f32) for span in spans],
            *[pltpu.VMEM((blocks - 1, 3, rows, span), f32) for span in spans * 2],
            dma((18,)),
            dma((2, blocks, most)),
            dma((2, blocks, most)),
            dma((2,)),
            dma((2,)),
            dma((2, 2)),
            dma((2, 2)),
            dma((2, 2, 2)),
            dma((2, 2, 2)),
            dma((2, blocks - 1, 2)),
            dma((2, blocks - 1, 2)),
        ],
        compiler_params=pltpu.CompilerParams(
            collective_id=0, has_side_effects=True, vmem_limit_bytes=56 * 1024 * 1024
        ),
    )(
        adj_u,
        adj_v,
        adj_zeta,
        saved_zeta,
        saved_ubar,
        stored_mean_north_velocity,
        depth,
        scaled_inverse_area,
        rho_mask,
        u_mask,
        v_mask,
        level_base,
        level_slope,
        filter_table,
        filter_index,
    )
    return pl.pallas_call(
        hand_out,
        out_shape=(flat, flat, flat, tall, tall),
        in_specs=[hbm],
        out_specs=(hbm,) * 5,
        scratch_shapes=[pltpu.VMEM((3 + 2 * levels, rows, columns), f32), dma((2, 5))],
    )(together)


def solution(mesh):
    placed = (
        P(None, "lat", "lon"),
        P(None, "lat", "lon"),
        P("lat", "lon"),
        P(None, "lat", "lon"),
        P(None, "lat", "lon"),
        P(None, "lat", "lon"),
        P("lat", "lon"),
        P("lat", "lon"),
        P(),
        P(),
        P("lat", "lon"),
        P("lat", "lon"),
        P("lat", "lon"),
        P(),
        P(),
    )
    return jax.shard_map(
        functools.partial(body, mesh.shape["lon"], mesh.shape["lat"]),
        mesh=mesh,
        in_specs=placed,
        out_specs=(
            P("lat", "lon"),
            P("lat", "lon"),
            P("lat", "lon"),
            P(None, "lat", "lon"),
            P(None, "lat", "lon"),
        ),
        check_vma=False,
    )
```
